128 devices in a mesh: replica: 8 (over z, x_lo), fsdp: 16 (over y, x_hi, core).
Axes of the slice: x: 4 (x_hi: 2, x_lo: 2; x = x_hi * 2 + x_lo), y: 4, z: 4, core: 2. Of those that a mesh axis runs over, the one named last changes fastest.
Arguments:
- codes: int32 [8, 3584, 7168], P('replica', None, 'fsdp'), may hold values from -8 to 7
- exponents: int32 [8, 28, 7168], P('replica', None, 'fsdp'), may hold values from -10 to -6
- params: float32 [3584, 7168], P('replica', 'fsdp'), may hold values from -0.09375 to 0.09375
- momentum: float32 [3584, 7168], P('replica', 'fsdp'), may hold values from -0.0625 to 0.0625
- attention: bfloat16 [8, 4096, 3584], P('replica', 'fsdp'), may hold values from -6 to 6
- residual: bfloat16 [8, 4096, 7168], P('replica', 'fsdp'), may hold values from -6 to 6
Outputs:
- params_out: float32 [3584, 7168], P('replica', 'fsdp')
- momentum_out: float32 [3584, 7168], P('replica', 'fsdp')
- hidden_out: bfloat16 [8, 4096, 7168], P('replica', 'fsdp')
The draws below stay inside these ranges and needn't reach their ends.
All inputs are finite; a program needn't handle non-finite values.
Results may differ from the reference program's by a relative error of at most 0.0075.
Values may be sent and summed in bfloat16 or wider, within the bound.
A program may use at most 128 MiB of HBM per device.

```python
import jax
import jax.numpy as jnp
from jax import lax

D = 7168
HEAD_FEATS = 3584
REPLICAS = 8
TOK_REP = 4096
BLOCKS = 28


def with_ends(array, stream_key, low, largest):
    shape = array.shape
    place = [jax.random.randint(jax.random.fold_in(stream_key, axis), (), 0, shape[axis]) for axis in range(len(shape))]
    array = array.at[tuple(place)].set(low)
    longest = shape.index(max(shape))
    place[longest] = (place[longest] + 1) % shape[longest]
    return array.at[tuple(place)].set(largest)


def block_levels(own_key, shape, cuts, least, high):
    level = 1.0
    for dim, blocks in cuts:
        heights = jax.random.uniform(jax.random.fold_in(jax.random.fold_in(own_key, 6), dim), (blocks,), jnp.float32, least / len(cuts), high / len(cuts))
        level = level * jnp.repeat(jnp.exp(heights), shape[dim] // blocks).reshape((-1,) + (1,) * (len(shape) - 1 - dim))
    return level


def centred(rng, dims, deviation, limit, cuts=(), kind=jnp.bfloat16):
    level = block_levels(rng, dims, cuts, -0.22, 0.18) if cuts else 1.0
    entries = jax.random.normal(rng, dims, jnp.float32) * deviation * level
    return jnp.minimum(jnp.maximum(entries, -limit), limit).astype(kind)


def setup_inputs(seed: int = 0) -> dict:
    key_of = jax.random.split(jax.random.key(seed), 7)
    codes = with_ends(jax.random.randint(key_of[0], (REPLICAS, HEAD_FEATS, D), -8, 8), jax.random.fold_in(key_of[0], 1), -8, 7).astype(jnp.int32)
    exponents = with_ends(jax.random.randint(key_of[1], (REPLICAS, BLOCKS, D), -10, -5), jax.random.fold_in(key_of[1], 1), -10, (-5) - 1).astype(jnp.int32)
    params = centred(key_of[2], (HEAD_FEATS, D), HEAD_FEATS ** -0.5, 0.09375, ((0, 8), (1, 16)), jnp.float32)
    momentum = centred(key_of[3], (HEAD_FEATS, D), 0.01, 0.0625, ((0, 8), (1, 16)), jnp.float32)
    attention = centred(key_of[4], (REPLICAS, TOK_REP, HEAD_FEATS), 1.0, 6.0, ((0, 8), (1, 16)))
    residual = centred(key_of[5], (REPLICAS, TOK_REP, D), 1.0, 6.0, ((0, 8), (1, 16)))
    return {"codes": codes, "exponents": exponents, "params": params, "momentum": momentum, "attention": attention, "residual": residual}


def scale_of(exponents):
    scales = jnp.zeros(exponents.shape, jnp.float32)
    for exponent_value in range(-10, -5):
        scales = scales + jnp.where(exponents == exponent_value, jnp.float32(2.0 ** exponent_value), jnp.float32(0.0))
    return scales


def dequantize(code_block, exponent_block):
    scales = scale_of(exponent_block)
    blocks = exponent_block.shape[0]
    width = code_block.shape[1]
    shaped = code_block.astype(jnp.float32).reshape(blocks, code_block.shape[0] // blocks, width)
    return (shaped * scales[:, None, :]).reshape(code_block.shape[0], width)


def reference(codes, exponents, params, momentum, attention, residual):
    def add_replica(summed, pieces):
        code_piece, exponent_piece = pieces
        return summed + dequantize(code_piece, exponent_piece), None

    summed, unused = lax.scan(add_replica, jnp.zeros(params.shape, jnp.float32), (codes, exponents))
    outer_grad = summed / REPLICAS
    momentum_out = 0.9 * momentum + outer_grad
    params_out = params - 0.7 * (outer_grad + 0.9 * momentum_out)
    out_weight = params_out.astype(jnp.bfloat16)

    def project(rows):
        return jnp.dot(rows, out_weight, preferred_element_type=jnp.float32).astype(jnp.bfloat16)

    projected = lax.optimization_barrier(lax.map(project, attention))
    hidden_out = (residual.astype(jnp.float32) + projected.astype(jnp.float32)).astype(jnp.bfloat16)
    return params_out, momentum_out, hidden_out
```

```python
import jax
import jax.numpy as jnp
from jax import lax
from jax.experimental import pallas as pl
from jax.experimental.pallas import tpu as pltpu
from jax.sharding import PartitionSpec as P

MESH = pl.DeviceIdType.MESH
F32, BF16 = jnp.float32, jnp.bfloat16

COLS = 448
KDIM = 3584
TOK = 256
PAIR = 896
PIECE = 224
SEND = 7 * PIECE


def scale_of(exponents):
    scales = jnp.zeros(exponents.shape, F32)
    for exponent_value in range(-10, -5):
        scales = scales + jnp.where(
            exponents == exponent_value, jnp.float32(2.0**exponent_value), jnp.float32(0.0)
        )
    return scales


def device(x, y, z, c):
    return (z * 2 + lax.rem(x, 2), (y * 2 + x // 2) * 2 + c)


def kernel(
    codes, scales, params, momentum, attention,
    params_out, momentum_out, projected,
    codes_v, deltas, received, par_v, mom_v, summed, block, block_in, weight, att, outs,
    local_sem, rs_s, rs_r, at_s, at_r, sw_s, sw_r, sib_s, sib_r, xs, xr, zs, zr, os_, or_,
):
    r = lax.axis_index("replica")
    f = lax.axis_index("fsdp")
    z, xl = r // 2, lax.rem(r, 2)
    y, xh, c = f // 4, lax.rem(f // 2, 2), lax.rem(f, 2)
    x = xh * 2 + xl
    xo = lax.rem(x + 3 + 2 * xl, 4)
    x2 = lax.rem(x + 2, 4)
    xp = xh * 2 + (1 - xl)
    zu, zd, z2 = lax.rem(z + 1, 4), lax.rem(z + 3, 4), lax.rem(z + 2, 4)
    yu, yd = lax.rem(y + 1, 4), lax.rem(y + 3, 4)
    sibling = device(x, y, z, 1 - c)
    to_xp, to_xo = device(xp, y, z, c), device(xo, y, z, c)
    to_zu, to_zd = device(x, y, zu, c), device(x, y, zd, c)
    to_yu, to_yd = device(x, yu, z, c), device(x, yd, z, c)

    barrier = pltpu.get_barrier_semaphore()
    partners = [sibling, to_xo, to_yu, to_yd, device(x, lax.rem(y + 2, 4), z, c), to_xp]
    for dz in (1, 2, 3):
        for there in (x, xp):
            partners.append(device(there, y, lax.rem(z + dz, 4), c))
    for partner in partners:
        pl.semaphore_signal(barrier, inc=1, device_id=partner, device_id_type=MESH)

    z_order = [z2, zu, zd, z]
    code_copies = []
    for i, zz in enumerate(z_order):
        copy = pltpu.make_async_copy(
            codes.at[:, pl.ds(pl.multiple_of(zz * PAIR, 128), PAIR)], codes_v.at[i], local_sem.at[i]
        )
        copy.start()
        code_copies.append(copy)
    par_copy = pltpu.make_async_copy(params, par_v, local_sem.at[4])
    mom_copy = pltpu.make_async_copy(momentum, mom_v, local_sem.at[5])
    att_copy = pltpu.make_async_copy(attention, att.at[y], local_sem.at[6])
    par_copy.start()
    mom_copy.start()
    att_copy.start()
    pl.semaphore_wait(barrier, len(partners))

    pending = []

    def send(src, dst, s, q, to):
        copy = pltpu.make_async_remote_copy(
            src_ref=src, dst_ref=dst, send_sem=s, recv_sem=q, device_id=to, device_id_type=MESH
        )
        copy.start()
        pending.append(copy)
        return copy

    half = TOK // 2
    low, high = pl.ds(0, half), pl.ds(half, half)
    at0 = send(attention.at[low], att.at[y, low], at_s.at[0], at_r.at[0], to_yu)
    at1 = send(attention.at[high], att.at[y, high], at_s.at[1], at_r.at[1], to_yd)

    lane = lax.broadcasted_iota(jnp.int32, (PIECE, 128), 1) < 64
    rs = []
    for i, zz in enumerate(z_order):
        code_copies[i].wait()
        scale = scales[zz]

        def tile(t):
            return codes_v[i, :, 128 * t : 128 * (t + 1)].astype(F32) * scale[:, t : t + 1]

        for t in range(3):
            deltas[2 * zz, t * COLS : (t + 1) * COLS] = tile(t).astype(BF16)
            deltas[2 * zz + 1, t * COLS : (t + 1) * COLS] = tile(t + 4).astype(BF16)
        mid = tile(3)
        turned = pltpu.roll(mid, 64, 1)
        top, bottom = mid[:PIECE], mid[PIECE:]
        deltas[2 * zz, 3 * COLS :] = jnp.where(lane, top, turned[PIECE:]).astype(BF16)
        deltas[2 * zz + 1, 3 * COLS :] = jnp.where(lane, turned[:PIECE], bottom).astype(BF16)
        for j, there in enumerate((xp, x)):
            if i == 3 and j == 1:
                continue
            k = 2 * i + j
            to = device(there, y, zz, c)
            rs.append(
                send(deltas.at[2 * zz + lax.rem(there, 2)], received.at[k], rs_s.at[k], rs_r.at[k], to)
            )

    att_copy.wait()
    at0.wait_recv()
    at2 = send(att.at[yd, low], att.at[yd, low], at_s.at[2], at_r.at[2], to_yu)
    at3 = send(att.at[y, high], att.at[y, high], at_s.at[3], at_r.at[3], to_yu)
    at1.wait_recv()
    at4 = send(att.at[yu, high], att.at[yu, high], at_s.at[4], at_r.at[4], to_yd)
    at5 = send(att.at[y, low], att.at[y, low], at_s.at[5], at_r.at[5], to_yd)

    for copy in rs:
        copy.wait_recv()

    def total(rows, size):
        acc = deltas[r, pl.ds(rows, size)].astype(F32)
        for k in range(7):
            acc = acc + received[k, pl.ds(rows, size)].astype(F32)
        return acc

    fill = jnp.zeros((64, 128), F32)
    for t in range(3):
        piece = jnp.concatenate([total(t * COLS, COLS), fill], axis=0).T
        summed[pl.ds(pl.multiple_of(xl * 64 + t * 128, 64), 128)] = piece[:, :COLS]
    packed = total(3 * COLS, PIECE)
    piece = jnp.concatenate([packed, pltpu.roll(packed, 64, 1), fill], axis=0).T
    summed[pl.ds(pl.multiple_of((1 - xl) * 384, 64), 64)] = piece[:64, :COLS]

    par_copy.wait()
    mom_copy.wait()
    outer_grad = summed[...] / 8
    new_momentum = 0.9 * mom_v[...] + outer_grad
    new_params = par_v[...] - 0.7 * (outer_grad + 0.9 * new_momentum)
    mom_v[...] = new_momentum
    par_v[...] = new_params
    block[...] = jnp.concatenate(
        [new_params, jnp.zeros((COLS, 64), F32)], axis=1
    ).astype(BF16)
    away = pl.ds(pl.multiple_of((1 - c) * PIECE, 16), PIECE)
    keep = pl.ds(pl.multiple_of(c * PIECE, 16), PIECE)
    swap = send(block.at[away], block_in, sw_s, sw_r, sibling)
    par_save = pltpu.make_async_copy(par_v, params_out, local_sem.at[4])
    mom_save = pltpu.make_async_copy(mom_v, momentum_out, local_sem.at[5])
    par_save.start()
    mom_save.start()
    swap.wait_recv()
    mine, other = block[keep].astype(F32), block_in[...].astype(F32)
    first = c == 0
    left = jnp.where(first, mine, other)
    right = pltpu.roll(jnp.where(first, other, mine), 64, 1)
    seam = jnp.where(lane, left[:, 384:], right[:, :128])
    own_rows = pl.ds(pl.multiple_of(r * COLS + c * PIECE, 16), PIECE)
    weight[xh, own_rows, :384] = left[:, :384].astype(BF16)
    weight[xh, own_rows, 384:512] = seam.astype(BF16)
    weight[xh, own_rows, 512:] = right[:, 128:].astype(BF16)

    def unit(x_, z_, part, lo=0, size=112):
        start = (2 * z_ + lax.rem(x_, 2)) * COLS + c * PIECE + part * 112 + lo
        return weight.at[x_ // 2, pl.ds(pl.multiple_of(start, 16), size)]

    shares = []

    def share(ref):
        k = len(shares)
        shares.append(send(ref, ref, sib_s.at[k], sib_r.at[k], sibling))
        return shares[-1]

    n_x, n_z = [0], [0]

    def along_x(ref, to):
        k = n_x[0]
        n_x[0] += 1
        return send(ref, ref, xs.at[k], xr.at[k], to)

    def along_z(ref, to):
        k = n_z[0]
        n_z[0] += 1
        return send(ref, ref, zs.at[k], zr.at[k], to)

    XP, XO, ZU, ZD = to_xp, to_xo, to_zu, to_zd
    own_shares, late_shares = [], []
    pz_u = along_z(unit(x, z, 0), ZU)
    pz_d = along_z(unit(x, z, 0), ZD)
    qx_p = along_x(unit(x, z, 1), XP)
    qx_o = along_x(unit(x, z, 1), XO)
    z_units = [z, zd, zu, z2]
    x_units = [x, xp, xo, x2]
    px_p, px_o, qz_u, qz_d = [], [], [], []
    px_p.append(along_x(unit(x, z, 0), XP))
    px_o.append(along_x(unit(x, z, 0), XO))
    qz_u.append(along_z(unit(x, z, 1), ZU))
    qz_d.append(along_z(unit(x, z, 1), ZD))
    own_shares.append(share(weight.at[xh, own_rows]))

    pz_u.wait_recv()
    pz2_u = along_z(unit(x, zd, 0, 0, 64), ZU)
    px_p.append(along_x(unit(x, zd, 0), XP))
    px_o.append(along_x(unit(x, zd, 0), XO))
    own_shares.append(share(unit(x, zd, 0)))
    pz_d.wait_recv()
    pz2_d = along_z(unit(x, zu, 0, 64, 48), ZD)
    px_p.append(along_x(unit(x, zu, 0), XP))
    px_o.append(along_x(unit(x, zu, 0), XO))
    own_shares.append(share(unit(x, zu, 0)))
    qx_p.wait_recv()
    qx2_o = along_x(unit(xp, z, 1, 0, 64), XO)
    qz_u.append(along_z(unit(xp, z, 1), ZU))
    qz_d.append(along_z(unit(xp, z, 1), ZD))
    own_shares.append(share(unit(xp, z, 1)))
    qx_o.wait_recv()
    qx2_p = along_x(unit(xo, z, 1, 64, 48), XP)
    qz_u.append(along_z(unit(xo, z, 1), ZU))
    qz_d.append(along_z(unit(xo, z, 1), ZD))
    late_shares.append(share(unit(xo, z, 1)))
    pz2_u.wait_recv()
    pz2_d.wait_recv()
    px_p.append(along_x(unit(x, z2, 0), XP))
    px_o.append(along_x(unit(x, z2, 0), XO))
    own_shares.append(share(unit(x, z2, 0)))
    qx2_o.wait_recv()
    qx2_p.wait_recv()
    qz_u.append(along_z(unit(x2, z, 1), ZU))
    qz_d.append(along_z(unit(x2, z, 1), ZD))
    late_shares.append(share(unit(x2, z, 1)))

    qz2 = [None] * 4

    def pass_z(j, bucket):
        qz_u[j].wait_recv()
        if j in (0, 2):
            qz2[j] = along_z(unit(x_units[j], zd, 1), ZU)
        bucket.append(share(unit(x_units[j], zd, 1)))
        qz_d[j].wait_recv()
        if j in (1, 3):
            qz2[j] = along_z(unit(x_units[j], zu, 1), ZD)
        bucket.append(share(unit(x_units[j], zu, 1)))

    px2 = [None] * 4
    pass_z(0, own_shares)
    pass_z(1, own_shares)
    for j in range(4):
        px_p[j].wait_recv()
        if j in (0, 1):
            px2[j] = along_x(unit(xp, z_units[j], 0), XO)
        own_shares.append(share(unit(xp, z_units[j], 0)))
        px_o[j].wait_recv()
        if j in (2, 3):
            px2[j] = along_x(unit(xo, z_units[j], 0), XP)
        late_shares.append(share(unit(xo, z_units[j], 0)))
    for j in (0, 1):
        qz2[j].wait_recv()
        own_shares.append(share(unit(x_units[j], z2, 1)))
    for copy in own_shares:
        copy.wait_recv()

    for copy in (at2, at3, at4, at5):
        copy.wait_recv()

    def multiply(side, begin, end):
        columns = xh if side == 0 else 1 - xh
        place = pl.ds(pl.multiple_of(y * 1792 + columns * PAIR, 128), PAIR)

        def step(i, carry):
            yy = lax.rem(y + 2 + i * (i + 1) // 2, 4)
            outs[side, i] = jnp.dot(
                att[yy], weight[columns], preferred_element_type=F32
            ).astype(BF16)

            @pl.when(i < 3)
            def _():
                pltpu.make_async_remote_copy(
                    src_ref=outs.at[side, i],
                    dst_ref=projected.at[:, place],
                    send_sem=os_.at[side, i],
                    recv_sem=or_.at[side, i],
                    device_id=device(x, yy, z, c),
                    device_id_type=MESH,
                ).start()

            @pl.when(i == 3)
            def _():
                pltpu.make_async_copy(
                    outs.at[side, i], projected.at[:, place], os_.at[side, i]
                ).start()

            return carry

        lax.fori_loop(begin, end, step, 0)
        return place

    place0 = multiply(0, 0, 2)
    pass_z(2, late_shares)
    pass_z(3, late_shares)
    multiply(0, 2, 4)
    for j in (0, 1, 2, 3):
        px2[j].wait_recv()
        late_shares.append(share(unit(x2, z_units[j], 0)))
    for j in (2, 3):
        qz2[j].wait_recv()
        late_shares.append(share(unit(x_units[j], z2, 1)))
    for copy in late_shares:
        copy.wait_recv()
    place1 = multiply(1, 0, 4)

    for copy in pending:
        copy.wait_send()
    par_save.wait()
    mom_save.wait()
    for side, place in ((0, place0), (1, place1)):
        pltpu.make_async_copy(outs.at[side, 3], projected.at[:, place], os_.at[side, 3]).wait()
        for i in range(3):
            out = pltpu.make_async_remote_copy(
                src_ref=outs.at[side, i],
                dst_ref=projected.at[:, place],
                send_sem=os_.at[side, i],
                recv_sem=or_.at[side, i],
                device_id=to_yu,
                device_id_type=MESH,
            )
            out.wait_send()
            out.wait_recv()


def shards(codes, exponents, params, momentum, attention, residual):
    scales = scale_of(exponents[0]).T.reshape(COLS, 4, 7).transpose(1, 0, 2)
    any_space = pl.BlockSpec(memory_space=pl.ANY)
    vmem = pl.BlockSpec(memory_space=pltpu.VMEM)
    dma = pltpu.SemaphoreType.DMA
    new_params, new_momentum, projected = pl.pallas_call(
        kernel,
        out_shape=(
            jax.ShapeDtypeStruct((COLS, COLS), F32),
            jax.ShapeDtypeStruct((COLS, COLS), F32),
            jax.ShapeDtypeStruct((TOK, 4 * 2 * PAIR), BF16),
        ),
        in_specs=[any_space, vmem, any_space, any_space, any_space],
        out_specs=(any_space, any_space, any_space),
        scratch_shapes=[
            pltpu.VMEM((4, COLS, PAIR), jnp.int32),
            pltpu.VMEM((8, SEND, 128), BF16),
            pltpu.VMEM((7, SEND, 128), BF16),
            pltpu.VMEM((COLS, COLS), F32),
            pltpu.VMEM((COLS, COLS), F32),
            pltpu.VMEM((COLS, COLS), F32),
            pltpu.VMEM((COLS, 512), BF16),
            pltpu.VMEM((PIECE, 512), BF16),
            pltpu.VMEM((2, KDIM, PAIR), BF16),
            pltpu.VMEM((4, TOK, KDIM), BF16),
            pltpu.VMEM((2, 4, TOK, PAIR), BF16),
            dma((7,)),
            dma((7,)), dma((7,)),
            dma((6,)), dma((6,)),
            dma, dma,
            dma((31,)), dma((31,)),
            dma((16,)), dma((16,)),
            dma((16,)), dma((16,)),
            dma((2, 4)), dma((2, 4)),
        ],
        compiler_params=pltpu.CompilerParams(
            collective_id=0, has_side_effects=True, vmem_limit_bytes=60 * 2**20
        ),
    )(jnp.swapaxes(codes[0], 0, 1), scales, params, momentum, attention[0])
    hidden_out = (residual[0].astype(F32) + projected.astype(F32)).astype(BF16)
    return (new_params, new_momentum, hidden_out[None])


def solution(mesh):
    placed = (
        P("replica", None, "fsdp"),
        P("replica", None, "fsdp"),
        P("replica", "fsdp"),
        P("replica", "fsdp"),
        P("replica", "fsdp", None),
        P("replica", "fsdp", None),
    )
    return jax.shard_map(
        shards,
        mesh=mesh,
        in_specs=placed,
        out_specs=(P("replica", "fsdp"), P("replica", "fsdp"), P("replica", "fsdp", None)),
        check_vma=False,
    )
```

```python
import jax
import jax.numpy as jnp
from jax import lax
from jax.experimental import pallas as pl
from jax.experimental.pallas import tpu as pltpu
from jax.sharding import PartitionSpec as P

MESH = pl.DeviceIdType.MESH
F32, BF16 = jnp.float32, jnp.bfloat16

COLS = 448
KDIM = 3584
TOK = 256
PAIR = 896
PIECE = 224
SEND = 7 * PIECE
VMEM_LIMIT = 48 * 2**20


def keep(array):
    return pltpu.with_memory_space_constraint(array, pltpu.HBM)


def scale_of(exponents):
    scales = jnp.zeros(exponents.shape, F32)
    for exponent_value in range(-10, -5):
        scales = scales + jnp.where(
            exponents == exponent_value, jnp.float32(2.0**exponent_value), jnp.float32(0.0)
        )
    return scales


def device(x, y, z, c):
    return (z * 2 + lax.rem(x, 2), (y * 2 + x // 2) * 2 + c)


def kernel(
    codes, exponents, params, momentum, attention, residual,
    params_out, momentum_out, hidden_out,
    codes_v, exp_v, deltas, received, par_v, mom_v, summed, block, block_in, weight, att, outs, got, hid,
    local_sem, rs_s, rs_r, at_s, at_r, sw_s, sw_r, sib_s, sib_r, xs, xr, zs, zr, os_, or_, save_sem,
):
    r = lax.axis_index("replica")
    f = lax.axis_index("fsdp")
    z, xl = r // 2, lax.rem(r, 2)
    y, xh, c = f // 4, lax.rem(f // 2, 2), lax.rem(f, 2)
    x = xh * 2 + xl
    xo = lax.rem(x + 3 + 2 * xl, 4)
    x2 = lax.rem(x + 2, 4)
    xp = xh * 2 + (1 - xl)
    zu, zd, z2 = lax.rem(z + 1, 4), lax.rem(z + 3, 4), lax.rem(z + 2, 4)
    yu, yd = lax.rem(y + 1, 4), lax.rem(y + 3, 4)
    sibling = device(x, y, z, 1 - c)
    to_xp, to_xo = device(xp, y, z, c), device(xo, y, z, c)
    to_zu, to_zd = device(x, y, zu, c), device(x, y, zd, c)
    to_yu, to_yd = device(x, yu, z, c), device(x, yd, z, c)

    barrier = pltpu.get_barrier_semaphore()
    partners = [sibling, to_xp, to_xo, to_yu, to_yd, device(x, lax.rem(y + 2, 4), z, c)]
    partners += [to_zu, to_zd, device(x, y, z2, c)]
    for partner in partners:
        pl.semaphore_signal(barrier, inc=1, device_id=partner, device_id_type=MESH)

    z_order = [z2, zu, zd, z]
    exp_copy = pltpu.make_async_copy(exponents, exp_v, local_sem.at[8])
    exp_copy.start()
    code_copies = []
    for i, zz in enumerate(z_order):
        copy = pltpu.make_async_copy(
            codes.at[:, pl.ds(pl.multiple_of(zz * PAIR, 128), PAIR)], codes_v.at[i], local_sem.at[i]
        )
        copy.start()
        code_copies.append(copy)
    par_copy = pltpu.make_async_copy(params, par_v, local_sem.at[4])
    mom_copy = pltpu.make_async_copy(momentum, mom_v, local_sem.at[5])
    att_copy = pltpu.make_async_copy(attention, att.at[y], local_sem.at[6])
    res_copy = pltpu.make_async_copy(residual, hid, local_sem.at[7])
    par_copy.start()
    mom_copy.start()
    att_copy.start()
    res_copy.start()
    pl.semaphore_wait(barrier, len(partners))

    pending = []

    def send(src, dst, s, q, to):
        copy = pltpu.make_async_remote_copy(
            src_ref=src, dst_ref=dst, send_sem=s, recv_sem=q, device_id=to, device_id_type=MESH
        )
        copy.start()
        pending.append(copy)
        return copy

    half = TOK // 2
    low, high = pl.ds(0, half), pl.ds(half, half)
    at0 = send(attention.at[low], att.at[y, low], at_s.at[0], at_r.at[0], to_yu)
    at1 = send(attention.at[high], att.at[y, high], at_s.at[1], at_r.at[1], to_yd)
    at3 = send(attention.at[high], att.at[y, high], at_s.at[3], at_r.at[3], to_yu)
    at5 = send(attention.at[low], att.at[y, low], at_s.at[5], at_r.at[5], to_yd)

    lane = lax.broadcasted_iota(jnp.int32, (PIECE, 128), 1) < 64
    rs, other = [], 1 - xl
    exp_copy.wait()
    for i, zz in enumerate(z_order):
        code_copies[i].wait()
        scale = [scale_of(exp_v[7 * zz + t]) for t in range(7)]
        scale = jnp.concatenate(scale + [jnp.zeros((1, COLS), F32)], axis=0)
        scale = jnp.concatenate([scale, jnp.zeros((8, 64), F32)], axis=1).T[:COLS]

        def tile(t):
            return codes_v[i, :, 128 * t : 128 * (t + 1)].astype(F32) * scale[:, t : t + 1]

        for t in range(3):
            deltas[2 * zz, t * COLS : (t + 1) * COLS] = tile(t).astype(BF16)
            deltas[2 * zz + 1, t * COLS : (t + 1) * COLS] = tile(t + 4).astype(BF16)
        mid = tile(3)
        turned = pltpu.roll(mid, 64, 1)
        top, bottom = mid[:PIECE], mid[PIECE:]
        deltas[2 * zz, 3 * COLS :] = jnp.where(lane, top, turned[PIECE:]).astype(BF16)
        deltas[2 * zz + 1, 3 * COLS :] = jnp.where(lane, turned[:PIECE], bottom).astype(BF16)
        if i == 0:
            pair = send(deltas.at[2 * zz + other], received.at[0], rs_s.at[0], rs_r.at[0], to_xp)
        elif i < 3:
            to = device(x, y, zz, c)
            rs.append(send(deltas.at[2 * zz + other], received.at[i], rs_s.at[i], rs_r.at[i], to))
            k = i + 2
            rs.append(send(deltas.at[2 * zz + xl], received.at[k], rs_s.at[k], rs_r.at[k], to))

    def add(place, slots):
        acc = deltas[place].astype(F32)
        for k in slots:
            acc = acc + received[k].astype(F32)
        deltas[place] = acc.astype(BF16)

    far, near = 2 * z2 + xl, 2 * z + other
    pair.wait_recv()
    add(far, (0,))
    rs.append(send(deltas.at[far], received.at[5], rs_s.at[5], rs_r.at[5], device(x, y, z2, c)))
    rs[0].wait_recv()
    rs[2].wait_recv()
    add(near, (1, 2))
    rs.append(send(deltas.at[near], received.at[6], rs_s.at[6], rs_r.at[6], to_xp))

    att_copy.wait()
    at0.wait_recv()
    at2 = send(att.at[yd, low], att.at[yd, low], at_s.at[2], at_r.at[2], to_yu)
    at1.wait_recv()
    at4 = send(att.at[yu, high], att.at[yu, high], at_s.at[4], at_r.at[4], to_yd)

    for copy in (rs[1], rs[3], rs[4], rs[5]):
        copy.wait_recv()

    def total(rows, size):
        acc = deltas[r, pl.ds(rows, size)].astype(F32)
        for k in range(3, 7):
            acc = acc + received[k, pl.ds(rows, size)].astype(F32)
        return acc

    fill = jnp.zeros((64, 128), F32)
    for t in range(3):
        piece = jnp.concatenate([total(t * COLS, COLS), fill], axis=0).T
        summed[pl.ds(pl.multiple_of(xl * 64 + t * 128, 64), 128)] = piece[:, :COLS]
    packed = total(3 * COLS, PIECE)
    piece = jnp.concatenate([packed, pltpu.roll(packed, 64, 1), fill], axis=0).T
    summed[pl.ds(pl.multiple_of((1 - xl) * 384, 64), 64)] = piece[:64, :COLS]

    par_copy.wait()
    mom_copy.wait()
    outer_grad = summed[...] / 8
    new_momentum = 0.9 * mom_v[...] + outer_grad
    new_params = par_v[...] - 0.7 * (outer_grad + 0.9 * new_momentum)
    mom_v[...] = new_momentum
    par_v[...] = new_params
    block[...] = jnp.concatenate(
        [new_params, jnp.zeros((COLS, 64), F32)], axis=1
    ).astype(BF16)
    away = pl.ds(pl.multiple_of((1 - c) * PIECE, 16), PIECE)
    keep = pl.ds(pl.multiple_of(c * PIECE, 16), PIECE)
    swap = send(block.at[away], block_in, sw_s, sw_r, sibling)
    par_save = pltpu.make_async_copy(par_v, params_out, local_sem.at[4])
    mom_save = pltpu.make_async_copy(mom_v, momentum_out, local_sem.at[5])
    par_save.start()
    mom_save.start()
    swap.wait_recv()
    mine, theirs = block[keep].astype(F32), block_in[...].astype(F32)
    first = c == 0
    left = jnp.where(first, mine, theirs)
    right = pltpu.roll(jnp.where(first, theirs, mine), 64, 1)
    seam = jnp.where(lane, left[:, 384:], right[:, :128])
    own_rows = pl.ds(pl.multiple_of(r * COLS + c * PIECE, 16), PIECE)
    weight[xh, own_rows, :384] = left[:, :384].astype(BF16)
    weight[xh, own_rows, 384:512] = seam.astype(BF16)
    weight[xh, own_rows, 512:] = right[:, 128:].astype(BF16)

    def unit(x_, z_, part, lo=0, size=112):
        start = (2 * z_ + lax.rem(x_, 2)) * COLS + c * PIECE + part * 112 + lo
        return weight.at[x_ // 2, pl.ds(pl.multiple_of(start, 16), size)]

    shares = []

    def share(ref):
        k = len(shares)
        shares.append(send(ref, ref, sib_s.at[k], sib_r.at[k], sibling))
        return shares[-1]

    n_x, n_z = [0], [0]

    def along_x(ref, to):
        k = n_x[0]
        n_x[0] += 1
        return send(ref, ref, xs.at[k], xr.at[k], to)

    def along_z(ref, to):
        k = n_z[0]
        n_z[0] += 1
        return send(ref, ref, zs.at[k], zr.at[k], to)

    XP, XO, ZU, ZD = to_xp, to_xo, to_zu, to_zd
    own_shares, late_shares = [], []
    pz_u = along_z(unit(x, z, 0), ZU)
    pz_d = along_z(unit(x, z, 0), ZD)
    qx_p = along_x(unit(x, z, 1), XP)
    qx_o = along_x(unit(x, z, 1), XO)
    z_units = [z, zd, zu, z2]
    x_units = [x, xp, xo, x2]
    px_p, px_o, qz_u, qz_d = [], [], [], []
    px_p.append(along_x(unit(x, z, 0), XP))
    px_o.append(along_x(unit(x, z, 0), XO))
    qz_u.append(along_z(unit(x, z, 1), ZU))
    qz_d.append(along_z(unit(x, z, 1), ZD))
    own_shares.append(share(weight.at[xh, own_rows]))

    def both(u, d, u_, d_):
        u.append(along_z(u_, ZU))
        d.append(along_z(d_, ZD))

    pz_u.wait_recv()
    pz2_u = along_z(unit(x, zd, 0, 0, 64), ZU)
    px_p.append(along_x(unit(x, zd, 0), XP))
    px_o.append(along_x(unit(x, zd, 0), XO))
    own_shares.append(share(unit(x, zd, 0)))
    pz_d.wait_recv()
    pz2_d = along_z(unit(x, zu, 0, 64, 48), ZD)
    px_p.append(along_x(unit(x, zu, 0), XP))
    px_o.append(along_x(unit(x, zu, 0), XO))
    own_shares.append(share(unit(x, zu, 0)))
    qx_p.wait_recv()
    both(qz_u, qz_d, unit(xp, z, 1), unit(xp, z, 1))
    own_shares.append(share(unit(xp, z, 1)))
    qx_o.wait_recv()
    late_shares.append(share(unit(xo, z, 1)))

    def got_z(j, bucket):
        qz_u[j].wait_recv()
        bucket.append(share(unit(x_units[j], zd, 1)))
        qz_d[j].wait_recv()
        bucket.append(share(unit(x_units[j], zu, 1)))

    def got_x(j):
        px_p[j].wait_recv()
        own_shares.append(share(unit(xp, z_units[j], 0)))
        px_o[j].wait_recv()
        late_shares.append(share(unit(xo, z_units[j], 0)))

    px2, qz2 = [None] * 4, [None] * 4
    got_z(0, own_shares)
    qz2[0] = along_z(unit(x, zd, 1), ZU)
    got_x(0)
    pz2_u.wait_recv()
    pz2_d.wait_recv()
    px_p.append(along_x(unit(x, z2, 0), XP))
    px_o.append(along_x(unit(x, z2, 0), XO))
    own_shares.append(share(unit(x, z2, 0)))
    qx2_o = along_x(unit(xp, z, 1, 0, 64), XO)
    qx2_p = along_x(unit(xo, z, 1, 64, 48), XP)
    got_x(1)
    px2[0] = along_x(unit(xp, z_units[0], 0), XO)
    px2[1] = along_x(unit(xp, z_units[1], 0), XO)
    got_z(1, own_shares)
    qz2[1] = along_z(unit(xp, zu, 1), ZD)
    both(qz_u, qz_d, unit(xo, z, 1), unit(xo, z, 1))
    got_x(2)
    px2[2] = along_x(unit(xo, z_units[2], 0), XP)
    for j in (0, 1):
        qz2[j].wait_recv()
        own_shares.append(share(unit(x_units[j], z2, 1)))
    got_x(3)
    px2[3] = along_x(unit(xo, z_units[3], 0), XP)
    for copy in own_shares:
        copy.wait_recv()

    for copy in (at2, at3, at4, at5):
        copy.wait_recv()

    def place(side, yy):
        columns = xh if side == 0 else 1 - xh
        return pl.ds(pl.multiple_of(yy * 1792 + columns * PAIR, 128), PAIR)

    def finish(side, i, value):
        here = place(side, lax.rem(y + 6 - i * (i + 1) // 2, 4))
        hid[:, here] = (hid[:, here].astype(F32) + value.astype(F32)).astype(BF16)
        pltpu.make_async_copy(
            hid.at[:, here], hidden_out.at[:, here], save_sem.at[side, i]
        ).start()

    def block_copy(side, i, to):
        return pltpu.make_async_remote_copy(
            src_ref=outs.at[side, i],
            dst_ref=got.at[side, i],
            send_sem=os_.at[side, i],
            recv_sem=or_.at[side, i],
            device_id=to,
            device_id_type=MESH,
        )

    def multiply(side, begin, end):
        columns = xh if side == 0 else 1 - xh

        def step(i, carry):
            yy = lax.rem(y + 2 + i * (i + 1) // 2, 4)
            result = jnp.dot(att[yy], weight[columns], preferred_element_type=F32).astype(BF16)

            @pl.when(i < 3)
            def _():
                outs[side, i] = result
                block_copy(side, i, device(x, yy, z, c)).start()

            @pl.when(i == 3)
            def _():
                finish(side, i, result)

            return carry

        lax.fori_loop(begin, end, step, 0)

    res_copy.wait()
    multiply(0, 0, 1)
    qx2_o.wait_recv()
    qx2_p.wait_recv()
    both(qz_u, qz_d, unit(x2, z, 1), unit(x2, z, 1))
    late_shares.append(share(unit(x2, z, 1)))
    got_z(2, late_shares)
    qz2[2] = along_z(unit(xo, zd, 1), ZU)
    multiply(0, 1, 3)
    got_z(3, late_shares)
    qz2[3] = along_z(unit(x2, zu, 1), ZD)
    multiply(0, 3, 4)
    for j in (0, 1, 2, 3):
        px2[j].wait_recv()
        late_shares.append(share(unit(x2, z_units[j], 0)))
    for j in (2, 3):
        qz2[j].wait_recv()
        late_shares.append(share(unit(x_units[j], z2, 1)))
    for copy in late_shares:
        copy.wait_recv()
    multiply(1, 0, 4)

    for side in range(2):

        def arrive(i, carry):
            block_copy(side, i, to_yu).wait_recv()
            finish(side, i, got[side, i])
            return carry

        lax.fori_loop(0, 3, arrive, 0)

    for copy in pending:
        copy.wait_send()
    par_save.wait()
    mom_save.wait()
    for side in range(2):
        for i in range(4):
            here = place(side, y)
            pltpu.make_async_copy(
                hid.at[:, here], hidden_out.at[:, here], save_sem.at[side, i]
            ).wait()
            if i < 3:
                block_copy(side, i, to_yu).wait_send()


def store(hidden, params, momentum, hidden_out, params_out, momentum_out, sem):
    copies = [
        pltpu.make_async_copy(params, params_out, sem.at[4]),
        pltpu.make_async_copy(momentum, momentum_out, sem.at[5]),
    ]
    for k in range(4):
        rows = pl.ds(k * TOK // 4, TOK // 4)
        copies.append(pltpu.make_async_copy(hidden.at[rows], hidden_out.at[rows], sem.at[k]))
    for copy in copies:
        copy.start()
    for copy in copies:
        copy.wait()


def shards(codes, exponents, params, momentum, attention, residual):
    any_space = pl.BlockSpec(memory_space=pl.ANY)
    dma = pltpu.SemaphoreType.DMA
    outer = jax.ShapeDtypeStruct((COLS, COLS), F32)
    hidden = jax.ShapeDtypeStruct((TOK, 4 * 2 * PAIR), BF16)
    new_params, new_momentum, new_hidden = pl.pallas_call(
        kernel,
        out_shape=(outer, outer, hidden),
        in_specs=[any_space] * 6,
        out_specs=(any_space, any_space, any_space),
        scratch_shapes=[
            pltpu.VMEM((4, COLS, PAIR), jnp.int32),
            pltpu.VMEM((4 * 7, 1, COLS), jnp.int32),
            pltpu.VMEM((8, SEND, 128), BF16),
            pltpu.VMEM((7, SEND, 128), BF16),
            pltpu.VMEM((COLS, COLS), F32),
            pltpu.VMEM((COLS, COLS), F32),
            pltpu.VMEM((COLS, COLS), F32),
            pltpu.VMEM((COLS, 512), BF16),
            pltpu.VMEM((PIECE, 512), BF16),
            pltpu.VMEM((2, KDIM, PAIR), BF16),
            pltpu.VMEM((4, TOK, KDIM), BF16),
            pltpu.VMEM((2, 3, TOK, PAIR), BF16),
            pltpu.VMEM((2, 3, TOK, PAIR), BF16),
            pltpu.VMEM((TOK, 4 * 2 * PAIR), BF16),
            dma((9,)),
            dma((7,)), dma((7,)),
            dma((6,)), dma((6,)),
            dma, dma,
            dma((31,)), dma((31,)),
            dma((16,)), dma((16,)),
            dma((16,)), dma((16,)),
            dma((2, 3)), dma((2, 3)),
            dma((2, 4)),
        ],
        compiler_params=pltpu.CompilerParams(
            collective_id=0, has_side_effects=True, vmem_limit_bytes=VMEM_LIMIT
        ),
    )(
        jnp.swapaxes(codes[0], 0, 1),
        keep(jnp.swapaxes(exponents, 0, 1)),
        *(keep(a) for a in (params, momentum, attention[0], residual[0])),
    )
    new_hidden, new_params, new_momentum = pl.pallas_call(
        store,
        out_shape=(hidden, outer, outer),
        in_specs=[any_space] * 3,
        out_specs=(any_space, any_space, any_space),
        scratch_shapes=[dma((6,))],
        compiler_params=pltpu.CompilerParams(vmem_limit_bytes=2**20),
    )(new_hidden, new_params, new_momentum)
    return (new_params, new_momentum, new_hidden[None])


def solution(mesh):
    placed = (
        P("replica", None, "fsdp"),
        P("replica", None, "fsdp"),
        P("replica", "fsdp"),
        P("replica", "fsdp"),
        P("replica", "fsdp", None),
        P("replica", "fsdp", None),
    )
    return jax.shard_map(
        shards,
        mesh=mesh,
        in_specs=placed,
        out_specs=(P("replica", "fsdp"), P("replica", "fsdp"), P("replica", "fsdp", None)),
        check_vma=False,
    )
```

```python
import jax
import jax.numpy as jnp
from jax import lax
from jax.experimental import pallas as pl
from jax.experimental.pallas import tpu as pltpu
from jax.sharding import PartitionSpec as P

MESH = pl.DeviceIdType.MESH
F32, BF16 = jnp.float32, jnp.bfloat16

COLS = 448
KDIM = 3584
TOK = 256
PAIR = 896
PIECE = 224
LATE = 128
EARLY = PAIR - LATE
SEND = 7 * PIECE
VMEM_LIMIT = 48 * 2**20


def keep(array):
    return pltpu.with_memory_space_constraint(array, pltpu.HBM)


def scale_of(exponents):
    scales = jnp.zeros(exponents.shape, F32)
    for exponent_value in range(-10, -5):
        scales = scales + jnp.where(
            exponents == exponent_value, jnp.float32(2.0**exponent_value), jnp.float32(0.0)
        )
    return scales


def device(x, y, z, c):
    return (z * 2 + lax.rem(x, 2), (y * 2 + x // 2) * 2 + c)


def kernel(
    codes, exponents, params, momentum, attention, residual,
    params_out, momentum_out, hidden_out,
    codes_v, exp_v, deltas, received, par_v, mom_v, block, block_in, weight, late, att, outs, got, hid,
    local_sem, rs_s, rs_r, at_s, at_r, sw_s, sw_r, sib_s, sib_r, late_s, late_r, xs, xr, zs, zr, os_, or_, save_sem, late_save,
):
    r = lax.axis_index("replica")
    f = lax.axis_index("fsdp")
    z, xl = r // 2, lax.rem(r, 2)
    y, xh, c = f // 4, lax.rem(f // 2, 2), lax.rem(f, 2)
    x = xh * 2 + xl
    xo = lax.rem(x + 3 + 2 * xl, 4)
    x2 = lax.rem(x + 2, 4)
    xp = xh * 2 + (1 - xl)
    zu, zd, z2 = lax.rem(z + 1, 4), lax.rem(z + 3, 4), lax.rem(z + 2, 4)
    yu, yd, y2 = lax.rem(y + 1, 4), lax.rem(y + 3, 4), lax.rem(y + 2, 4)
    sibling = device(x, y, z, 1 - c)
    to_xp, to_xo = device(xp, y, z, c), device(xo, y, z, c)
    to_zu, to_zd = device(x, y, zu, c), device(x, y, zd, c)
    to_yu, to_yd = device(x, yu, z, c), device(x, yd, z, c)

    barrier = pltpu.get_barrier_semaphore()
    partners = [sibling, to_xp, to_xo, to_yu, to_yd, device(x, y2, z, c)]
    partners += [to_zu, to_zd, device(x, y, z2, c), device(x2, y, z, c)]
    for partner in partners:
        pl.semaphore_signal(barrier, inc=1, device_id=partner, device_id_type=MESH)

    z_order = [z2, zu, zd, z]
    exp_copy = pltpu.make_async_copy(exponents, exp_v, local_sem.at[8])
    exp_copy.start()
    code_copies = [
        pltpu.make_async_copy(
            codes.at[pl.ds(h % 2 * PIECE, PIECE), pl.ds(pl.multiple_of(z_order[h // 2] * PAIR, 128), PAIR)],
            codes_v.at[h % 3],
            local_sem.at[9 + h],
        )
        for h in range(8)
    ]
    for copy in code_copies[:3]:
        copy.start()
    par_copy = pltpu.make_async_copy(params, par_v, local_sem.at[4])
    mom_copy = pltpu.make_async_copy(momentum, mom_v, local_sem.at[5])
    att_copy = pltpu.make_async_copy(attention, att.at[y], local_sem.at[6])
    res_copy = pltpu.make_async_copy(residual, hid, local_sem.at[7])
    par_copy.start()
    mom_copy.start()
    att_copy.start()
    res_copy.start()
    pl.semaphore_wait(barrier, len(partners))

    pending = []

    def send(src, dst, s, q, to):
        copy = pltpu.make_async_remote_copy(
            src_ref=src, dst_ref=dst, send_sem=s, recv_sem=q, device_id=to, device_id_type=MESH
        )
        copy.start()
        pending.append(copy)
        return copy

    half = TOK // 2
    low, high = pl.ds(0, half), pl.ds(half, half)
    at0 = send(attention.at[low], att.at[y, low], at_s.at[0], at_r.at[0], to_yu)
    at1 = send(attention.at[high], att.at[y, high], at_s.at[1], at_r.at[1], to_yd)
    at3 = send(attention.at[high], att.at[y, high], at_s.at[3], at_r.at[3], to_yu)
    at5 = send(attention.at[low], att.at[y, low], at_s.at[5], at_r.at[5], to_yd)

    lane = lax.broadcasted_iota(jnp.int32, (PIECE, 128), 1) < 64
    rs, other = [], 1 - xl
    exp_copy.wait()
    for i, zz in enumerate(z_order):
        scale = [scale_of(exp_v[7 * zz + t]) for t in range(7)]
        scale = jnp.concatenate(scale + [jnp.zeros((1, COLS), F32)], axis=0)
        scale = jnp.concatenate([scale, jnp.zeros((8, 64), F32)], axis=1).T[:COLS]

        middles = []
        for h in (2 * i, 2 * i + 1):
            first_col = h % 2 * PIECE
            code_copies[h].wait()

            def tile(t):
                code = codes_v[h % 3, :, 128 * t : 128 * (t + 1)].astype(F32)
                return code * scale[first_col : first_col + PIECE, t : t + 1]

            for t in range(3):
                rows = slice(t * COLS + first_col, t * COLS + first_col + PIECE)
                deltas[2 * zz, rows] = tile(t).astype(BF16)
                deltas[2 * zz + 1, rows] = tile(t + 4).astype(BF16)
            middles.append(tile(3))
            if h + 3 < 8:
                code_copies[h + 3].start()
        top, bottom = middles
        deltas[2 * zz, 3 * COLS :] = jnp.where(lane, top, pltpu.roll(bottom, 64, 1)).astype(BF16)
        deltas[2 * zz + 1, 3 * COLS :] = jnp.where(lane, pltpu.roll(top, 64, 1), bottom).astype(BF16)
        if i == 0:
            pair = send(deltas.at[2 * zz + other], received.at[0], rs_s.at[0], rs_r.at[0], to_xp)
        elif i < 3:
            to = device(x, y, zz, c)
            rs.append(send(deltas.at[2 * zz + other], received.at[i], rs_s.at[i], rs_r.at[i], to))
            k = i + 2
            rs.append(send(deltas.at[2 * zz + xl], received.at[k], rs_s.at[k], rs_r.at[k], to))

    def add(place, slots):
        acc = deltas[place].astype(F32)
        for k in slots:
            acc = acc + received[k].astype(F32)
        deltas[place] = acc.astype(BF16)

    far, near = 2 * z2 + xl, 2 * z + other
    pair.wait_recv()
    add(far, (0,))
    rs.append(send(deltas.at[far], received.at[5], rs_s.at[5], rs_r.at[5], device(x, y, z2, c)))
    rs[0].wait_recv()
    rs[2].wait_recv()
    add(near, (1, 2))
    rs.append(send(deltas.at[near], received.at[6], rs_s.at[6], rs_r.at[6], to_xp))

    for copy in (rs[1], rs[3], rs[4], rs[5]):
        copy.wait_recv()

    def total(rows, size):
        acc = deltas[r, pl.ds(rows, size)].astype(F32)
        for k in range(3, 7):
            acc = acc + received[k, pl.ds(rows, size)].astype(F32)
        return acc

    par_copy.wait()
    mom_copy.wait()

    def outer_step(rows, piece, size):
        outer_grad = piece[:size, :COLS] / 8
        new_momentum = 0.9 * mom_v[rows] + outer_grad
        new_params = par_v[rows] - 0.7 * (outer_grad + 0.9 * new_momentum)
        mom_v[rows] = new_momentum
        par_v[rows] = new_params
        block[rows] = jnp.concatenate(
            [new_params, jnp.zeros((size, 64), F32)], axis=1
        ).astype(BF16)

    fill = jnp.zeros((64, 128), F32)
    for t in range(3):
        piece = jnp.concatenate([total(t * COLS, COLS), fill], axis=0).T
        outer_step(pl.ds(pl.multiple_of(xl * 64 + t * 128, 64), 128), piece, 128)
    packed = total(3 * COLS, PIECE)
    piece = jnp.concatenate([packed, pltpu.roll(packed, 64, 1), fill], axis=0).T
    outer_step(pl.ds(pl.multiple_of((1 - xl) * 384, 64), 64), piece, 64)
    away = pl.ds(pl.multiple_of((1 - c) * PIECE, 16), PIECE)
    swap = send(block.at[away], block_in, sw_s, sw_r, sibling)
    par_save = pltpu.make_async_copy(par_v, params_out, local_sem.at[4])
    mom_save = pltpu.make_async_copy(mom_v, momentum_out, local_sem.at[5])
    par_save.start()
    mom_save.start()
    swap.wait_recv()
    first = c == 0
    seam_lane = lax.broadcasted_iota(jnp.int32, (112, 128), 1) < 64
    lanes = pl.ds(pl.multiple_of(xh * LATE, 128), LATE)
    own_rows = pl.ds(pl.multiple_of(r * COLS + c * PIECE, 16), PIECE)
    for part in range(2):
        ours = block[pl.ds(pl.multiple_of(c * PIECE + part * 112, 16), 112)].astype(F32)
        theirs = block_in[pl.ds(part * 112, 112)].astype(F32)
        left = jnp.where(first, ours, theirs)
        right = pltpu.roll(jnp.where(first, theirs, ours), 64, 1)
        seam = jnp.where(seam_lane, left[:, 384:], right[:, :128])
        rows = pl.ds(pl.multiple_of(r * COLS + c * PIECE + part * 112, 16), 112)
        weight[xh, rows, :384] = left[:, :384].astype(BF16)
        weight[xh, rows, 384:512] = seam.astype(BF16)
        weight[xh, rows, 512:] = right[:, 128 : EARLY - 384].astype(BF16)
        late[y, z, xl, 2 * c + part, :, lanes] = right[:, EARLY - 384 :].astype(BF16)

    def unit(x_, z_, part, lo=0, size=112):
        start = (2 * z_ + lax.rem(x_, 2)) * COLS + c * PIECE + part * 112 + lo
        return weight.at[x_ // 2, pl.ds(pl.multiple_of(start, 16), size)]

    shares = []

    def share(ref):
        k = len(shares)
        shares.append(send(ref, ref, sib_s.at[k], sib_r.at[k], sibling))
        return shares[-1]

    n_x, n_z = [0], [0]

    def along_x(ref, to):
        k = n_x[0]
        n_x[0] += 1
        return send(ref, ref, xs.at[k], xr.at[k], to)

    def along_z(ref, to):
        k = n_z[0]
        n_z[0] += 1
        return send(ref, ref, zs.at[k], zr.at[k], to)

    def late_send(k, ref, to):
        return send(ref, ref, late_s.at[k], late_r.at[k], to)

    to_y2, to_z2, to_x2 = device(x, y2, z, c), device(x, y, z2, c), device(x2, y, z, c)
    mine = pl.ds(pl.multiple_of(2 * c, 2), 2)
    late_y = [
        late_send(k, late.at[y, z, xl, mine, :, lanes], to)
        for k, to in enumerate((to_yu, to_yd, to_y2))
    ]

    XP, XO, ZU, ZD = to_xp, to_xo, to_zu, to_zd
    own_shares, late_shares = [], []
    pz_u = along_z(unit(x, z, 0), ZU)
    pz_d = along_z(unit(x, z, 0), ZD)
    qx_p = along_x(unit(x, z, 1), XP)
    qx_o = along_x(unit(x, z, 1), XO)
    z_units = [z, zd, zu, z2]
    x_units = [x, xp, xo, x2]
    px_p, px_o, qz_u, qz_d = [], [], [], []
    px_p.append(along_x(unit(x, z, 0), XP))
    px_o.append(along_x(unit(x, z, 0), XO))
    qz_u.append(along_z(unit(x, z, 1), ZU))
    qz_d.append(along_z(unit(x, z, 1), ZD))
    own_shares.append(share(weight.at[xh, own_rows]))

    def both(u, d, u_, d_):
        u.append(along_z(u_, ZU))
        d.append(along_z(d_, ZD))

    att_copy.wait()
    at0.wait_recv()
    at2 = send(att.at[yd, low], att.at[yd, low], at_s.at[2], at_r.at[2], to_yu)
    at1.wait_recv()
    at4 = send(att.at[yu, high], att.at[yu, high], at_s.at[4], at_r.at[4], to_yd)

    pz_u.wait_recv()
    pz2_u = along_z(unit(x, zd, 0, 0, 64), ZU)
    px_p.append(along_x(unit(x, zd, 0), XP))
    px_o.append(along_x(unit(x, zd, 0), XO))
    own_shares.append(share(unit(x, zd, 0)))
    pz_d.wait_recv()
    pz2_d = along_z(unit(x, zu, 0, 64, 48), ZD)
    px_p.append(along_x(unit(x, zu, 0), XP))
    px_o.append(along_x(unit(x, zu, 0), XO))
    own_shares.append(share(unit(x, zu, 0)))
    qx_p.wait_recv()
    both(qz_u, qz_d, unit(xp, z, 1), unit(xp, z, 1))
    own_shares.append(share(unit(xp, z, 1)))
    qx_o.wait_recv()
    late_shares.append(share(unit(xo, z, 1)))

    def got_z(j, bucket):
        qz_u[j].wait_recv()
        bucket.append(share(unit(x_units[j], zd, 1)))
        qz_d[j].wait_recv()
        bucket.append(share(unit(x_units[j], zu, 1)))

    def got_x(j):
        px_p[j].wait_recv()
        own_shares.append(share(unit(xp, z_units[j], 0)))
        px_o[j].wait_recv()
        late_shares.append(share(unit(xo, z_units[j], 0)))

    px2, qz2 = [None] * 4, [None] * 4
    got_z(0, own_shares)
    qz2[0] = along_z(unit(x, zd, 1), ZU)
    got_x(0)
    pz2_u.wait_recv()
    pz2_d.wait_recv()
    px_p.append(along_x(unit(x, z2, 0), XP))
    px_o.append(along_x(unit(x, z2, 0), XO))
    own_shares.append(share(unit(x, z2, 0)))
    qx2_o = along_x(unit(xp, z, 1, 0, 64), XO)
    qx2_p = along_x(unit(xo, z, 1, 64, 48), XP)
    got_x(1)
    px2[0] = along_x(unit(xp, z_units[0], 0), XO)
    px2[1] = along_x(unit(xp, z_units[1], 0), XO)
    got_z(1, own_shares)
    qz2[1] = along_z(unit(xp, zu, 1), ZD)
    both(qz_u, qz_d, unit(xo, z, 1), unit(xo, z, 1))
    got_x(2)
    px2[2] = along_x(unit(xo, z_units[2], 0), XP)
    for j in (0, 1):
        qz2[j].wait_recv()
        own_shares.append(share(unit(x_units[j], z2, 1)))
    got_x(3)
    px2[3] = along_x(unit(xo, z_units[3], 0), XP)
    for copy in own_shares:
        copy.wait_recv()

    for copy in (at3, at5):
        copy.wait_recv()

    def place(side, yy):
        columns = xh if side == 0 else 1 - xh
        return pl.ds(pl.multiple_of(yy * 1792 + columns * PAIR, 128), EARLY)

    def finish(side, i, value):
        here = place(side, lax.rem(y + 11 - 2 * i - i // 2, 4))
        for k in range(0, EARLY, 256):
            part = pl.ds(pl.multiple_of(here.start + k, 128), 256)
            total = hid[:, part].astype(F32) + value[:, k : k + 256].astype(F32)
            hid[:, part] = total.astype(BF16)
        pltpu.make_async_copy(
            hid.at[:, here], hidden_out.at[:, here], save_sem.at[side, i]
        ).start()

    def block_copy(side, i, to):
        return pltpu.make_async_remote_copy(
            src_ref=outs.at[side, i],
            dst_ref=got.at[side, i],
            send_sem=os_.at[side, i],
            recv_sem=or_.at[side, i],
            device_id=to,
            device_id_type=MESH,
        )

    def multiply(side, begin, end):
        columns = xh if side == 0 else 1 - xh

        def step(i, carry):
            yy = lax.rem(y + 1 + 2 * i + i // 2, 4)
            result = jnp.dot(att[yy], weight[columns], preferred_element_type=F32).astype(BF16)

            @pl.when(i < 3)
            def _():
                outs[side, i] = result
                block_copy(side, i, device(x, yy, z, c)).start()

            @pl.when(i == 3)
            def _():
                finish(side, i, result)

            return carry

        lax.fori_loop(begin, end, step, 0)

    res_copy.wait()
    for copy in late_y:
        copy.wait_recv()
    late_z = [
        late_send(3 + k, late.at[:, z, xl, 2 * c, :, lanes], to)
        for k, to in enumerate((to_zu, to_zd, to_z2))
    ]
    late_x = [
        late_send(6 + k, late.at[:, z, xl, 2 * c + 1, :, lanes], to)
        for k, to in enumerate((to_xp, to_xo, to_x2))
    ]
    multiply(0, 0, 1)
    qx2_o.wait_recv()
    qx2_p.wait_recv()
    both(qz_u, qz_d, unit(x2, z, 1), unit(x2, z, 1))
    late_shares.append(share(unit(x2, z, 1)))
    got_z(2, late_shares)
    qz2[2] = along_z(unit(xo, zd, 1), ZU)
    multiply(0, 1, 2)
    got_z(3, late_shares)
    qz2[3] = along_z(unit(x2, zu, 1), ZD)
    at2.wait_recv()
    at4.wait_recv()
    multiply(0, 2, 4)
    for copy in late_z:
        copy.wait_recv()
    late_zx = [
        late_send(9 + k, late.at[:, :, xl, 2 * c, :, lanes], to)
        for k, to in enumerate((to_xp, to_xo))
    ]
    late_pairs = [late_send(17, late.at[:, :, xl, 2 * c, :, lanes], sibling)]
    for copy in late_x:
        copy.wait_recv()
    late_xz = [
        late_send(11 + k, late.at[:, z, :, 2 * c + 1], to)
        for k, to in enumerate((to_zu, to_zd))
    ]
    late_pairs.append(late_send(18, late.at[:, z, :, 2 * c + 1], sibling))

    for j in (0, 1, 2, 3):
        px2[j].wait_recv()
        late_shares.append(share(unit(x2, z_units[j], 0)))
    for j in (2, 3):
        qz2[j].wait_recv()
        late_shares.append(share(unit(x_units[j], z2, 1)))
    for copy in late_shares:
        copy.wait_recv()
    multiply(1, 0, 4)

    def late_x_unit(x_, lo, size):
        there = pl.ds(pl.multiple_of(x_ // 2 * LATE, 128), LATE)
        return late.at[:, lo : lo + size, lax.rem(x_, 2), 2 * c, :, there]

    def late_z_unit(z_, lo, size):
        return late.at[lo : lo + size, z_, :, 2 * c + 1]

    late_zx[0].wait_recv()
    fx0 = late_send(13, late_x_unit(xp, 0, 2), to_xo)
    late_pairs.append(late_send(19, late_x_unit(xp, 0, 4), sibling))
    late_zx[1].wait_recv()
    fx1 = late_send(14, late_x_unit(xo, 2, 2), to_xp)
    late_pairs.append(late_send(20, late_x_unit(xo, 0, 4), sibling))
    late_xz[0].wait_recv()
    fz0 = late_send(15, late_z_unit(zd, 0, 2), to_zu)
    late_pairs.append(late_send(21, late_z_unit(zd, 0, 4), sibling))
    late_xz[1].wait_recv()
    fz1 = late_send(16, late_z_unit(zu, 2, 2), to_zd)
    late_pairs.append(late_send(22, late_z_unit(zu, 0, 4), sibling))

    def arrive(side):
        def step(i, carry):
            block_copy(side, i, to_yu).wait_recv()
            finish(side, i, got[side, i])
            return carry

        lax.fori_loop(0, 3, step, 0)

    arrive(0)
    for copy in (fx0, fx1):
        copy.wait_recv()
    late_pairs.append(late_send(23, late_x_unit(x2, 0, 4), sibling))
    for copy in (fz0, fz1):
        copy.wait_recv()
    late_pairs.append(late_send(24, late_z_unit(z2, 0, 4), sibling))
    for copy in late_pairs:
        copy.wait_recv()

    def late_step(yy, carry):
        result = jnp.zeros((TOK, 2 * LATE), F32)
        for k in range(4):
            result = result + jnp.dot(
                att[y, :, k * PAIR : (k + 1) * PAIR],
                late[yy, k].reshape(PAIR, 2 * LATE),
                preferred_element_type=F32,
            )
        result = result.astype(BF16)
        for k in range(2):
            here = pl.ds(pl.multiple_of(yy * 1792 + k * PAIR + EARLY, 128), LATE)
            value = result[:, k * LATE : (k + 1) * LATE].astype(F32)
            hid[:, here] = (hid[:, here].astype(F32) + value).astype(BF16)
            pltpu.make_async_copy(
                hid.at[:, here], hidden_out.at[:, here], late_save.at[yy, k]
            ).start()
        return carry

    lax.fori_loop(0, 4, late_step, 0)
    arrive(1)

    for copy in pending:
        copy.wait_send()
    par_save.wait()
    mom_save.wait()
    for side in range(2):
        for i in range(4):
            here = place(side, y)
            pltpu.make_async_copy(
                hid.at[:, here], hidden_out.at[:, here], save_sem.at[side, i]
            ).wait()
            if i < 3:
                block_copy(side, i, to_yu).wait_send()
            there = pl.ds(i * 1792 + side * PAIR + EARLY, LATE)
            pltpu.make_async_copy(
                hid.at[:, there], hidden_out.at[:, there], late_save.at[i, side]
            ).wait()


def store(hidden, params, momentum, hidden_out, params_out, momentum_out, sem):
    copies = [
        pltpu.make_async_copy(params, params_out, sem.at[4]),
        pltpu.make_async_copy(momentum, momentum_out, sem.at[5]),
    ]
    for k in range(4):
        rows = pl.ds(k * TOK // 4, TOK // 4)
        copies.append(pltpu.make_async_copy(hidden.at[rows], hidden_out.at[rows], sem.at[k]))
    for copy in copies:
        copy.start()
    for copy in copies:
        copy.wait()


def shards(codes, exponents, params, momentum, attention, residual):
    any_space = pl.BlockSpec(memory_space=pl.ANY)
    dma = pltpu.SemaphoreType.DMA
    outer = jax.ShapeDtypeStruct((COLS, COLS), F32)
    hidden = jax.ShapeDtypeStruct((TOK, 4 * 2 * PAIR), BF16)
    new_params, new_momentum, new_hidden = pl.pallas_call(
        kernel,
        out_shape=(outer, outer, hidden),
        in_specs=[any_space] * 6,
        out_specs=(any_space, any_space, any_space),
        scratch_shapes=[
            pltpu.VMEM((3, PIECE, PAIR), jnp.int32),
            pltpu.VMEM((4 * 7, 1, COLS), jnp.int32),
            pltpu.VMEM((8, SEND, 128), BF16),
            pltpu.VMEM((7, SEND, 128), BF16),
            pltpu.VMEM((COLS, COLS), F32),
            pltpu.VMEM((COLS, COLS), F32),
            pltpu.VMEM((COLS, 512), BF16),
            pltpu.VMEM((PIECE, 512), BF16),
            pltpu.VMEM((2, KDIM, EARLY), BF16),
            pltpu.VMEM((4, 4, 2, 4, 112, 2 * LATE), BF16),
            pltpu.VMEM((4, TOK, KDIM), BF16),
            pltpu.VMEM((2, 3, TOK, EARLY), BF16),
            pltpu.VMEM((2, 3, TOK, EARLY), BF16),
            pltpu.VMEM((TOK, 4 * 2 * PAIR), BF16),
            dma((17,)),
            dma((7,)), dma((7,)),
            dma((6,)), dma((6,)),
            dma, dma,
            dma((31,)), dma((31,)),
            dma((25,)), dma((25,)),
            dma((16,)), dma((16,)),
            dma((16,)), dma((16,)),
            dma((2, 3)), dma((2, 3)),
            dma((2, 4)),
            dma((4, 2)),
        ],
        compiler_params=pltpu.CompilerParams(
            collective_id=0, has_side_effects=True, vmem_limit_bytes=VMEM_LIMIT
        ),
    )(
        jnp.swapaxes(codes[0], 0, 1),
        keep(jnp.swapaxes(exponents, 0, 1)),
        *(keep(a) for a in (params, momentum, attention[0], residual[0])),
    )
    new_hidden, new_params, new_momentum = pl.pallas_call(
        store,
        out_shape=(hidden, outer, outer),
        in_specs=[any_space] * 3,
        out_specs=(any_space, any_space, any_space),
        scratch_shapes=[dma((6,))],
        compiler_params=pltpu.CompilerParams(vmem_limit_bytes=2**20),
    )(new_hidden, new_params, new_momentum)
    return (new_params, new_momentum, new_hidden[None])


def solution(mesh):
    placed = (
        P("replica", None, "fsdp"),
        P("replica", None, "fsdp"),
        P("replica", "fsdp"),
        P("replica", "fsdp"),
        P("replica", "fsdp", None),
        P("replica", "fsdp", None),
    )
    return jax.shard_map(
        shards,
        mesh=mesh,
        in_specs=placed,
        out_specs=(P("replica", "fsdp"), P("replica", "fsdp"), P("replica", "fsdp", None)),
        check_vma=False,
    )
```

```python
import jax
import jax.numpy as jnp
from jax import lax
from jax.experimental import pallas as pl
from jax.experimental.pallas import tpu as pltpu
from jax.sharding import PartitionSpec as P

MESH = pl.DeviceIdType.MESH
F32, BF16 = jnp.float32, jnp.bfloat16

COLS = 448
KDIM = 3584
TOK = 256
PAIR = 896
PIECE = 224
LATE = 128
EARLY = PAIR - LATE
SEND = 7 * PIECE
VMEM_LIMIT = 48 * 2**20


def keep(array):
    return pltpu.with_memory_space_constraint(array, pltpu.HBM)


def scale_of(exponents):
    scales = jnp.zeros(exponents.shape, F32)
    for exponent_value in range(-10, -5):
        scales = scales + jnp.where(
            exponents == exponent_value, jnp.float32(2.0**exponent_value), jnp.float32(0.0)
        )
    return scales


def device(x, y, z, c):
    return (z * 2 + lax.rem(x, 2), (y * 2 + x // 2) * 2 + c)


def kernel(
    codes, exponents, params, momentum, attention, residual,
    params_out, momentum_out, hidden_out,
    codes_v, exp_v, deltas, received, par_v, mom_v, block, block_in, weight, late, att, outs, got, hid,
    local_sem, rs_s, rs_r, at_s, at_r, sw_s, sw_r, sib_s, sib_r, late_s, late_r, xs, xr, zs, zr, os_, or_, save_sem, late_save,
):
    r = lax.axis_index("replica")
    f = lax.axis_index("fsdp")
    z, xl = r // 2, lax.rem(r, 2)
    y, xh, c = f // 4, lax.rem(f // 2, 2), lax.rem(f, 2)
    x = xh * 2 + xl
    xo = lax.rem(x + 3 + 2 * xl, 4)
    x2 = lax.rem(x + 2, 4)
    xp = xh * 2 + (1 - xl)
    zu, zd, z2 = lax.rem(z + 1, 4), lax.rem(z + 3, 4), lax.rem(z + 2, 4)
    yu, yd, y2 = lax.rem(y + 1, 4), lax.rem(y + 3, 4), lax.rem(y + 2, 4)
    sibling = device(x, y, z, 1 - c)
    to_xp, to_xo = device(xp, y, z, c), device(xo, y, z, c)
    to_zu, to_zd = device(x, y, zu, c), device(x, y, zd, c)
    to_yu, to_yd = device(x, yu, z, c), device(x, yd, z, c)

    barrier = pltpu.get_barrier_semaphore()
    partners = [sibling, to_xp, to_xo, to_yu, to_yd, device(x, y2, z, c)]
    partners += [to_zu, to_zd, device(x, y, z2, c), device(x2, y, z, c)]
    for partner in partners:
        pl.semaphore_signal(barrier, inc=1, device_id=partner, device_id_type=MESH)

    z_order = [z2, zu, zd, z]
    exp_copy = pltpu.make_async_copy(exponents, exp_v, local_sem.at[8])
    exp_copy.start()
    code_copies = [
        pltpu.make_async_copy(
            codes.at[pl.ds(h % 2 * PIECE, PIECE), pl.ds(pl.multiple_of(z_order[h // 2] * PAIR, 128), PAIR)],
            codes_v.at[h % 3],
            local_sem.at[9 + h],
        )
        for h in range(8)
    ]
    for copy in code_copies[:3]:
        copy.start()
    par_copy = pltpu.make_async_copy(params, par_v, local_sem.at[4])
    mom_copy = pltpu.make_async_copy(momentum, mom_v, local_sem.at[5])
    att_copy = pltpu.make_async_copy(attention, att.at[y], local_sem.at[6])
    res_copy = pltpu.make_async_copy(residual, hid, local_sem.at[7])
    par_copy.start()
    mom_copy.start()
    att_copy.start()
    res_copy.start()
    pl.semaphore_wait(barrier, len(partners))

    pending = []

    def send(src, dst, s, q, to):
        copy = pltpu.make_async_remote_copy(
            src_ref=src, dst_ref=dst, send_sem=s, recv_sem=q, device_id=to, device_id_type=MESH
        )
        copy.start()
        pending.append(copy)
        return copy

    half = TOK // 2
    low, high = pl.ds(0, half), pl.ds(half, half)
    at0 = send(attention.at[low], att.at[y, low], at_s.at[0], at_r.at[0], to_yu)
    at1 = send(attention.at[high], att.at[y, high], at_s.at[1], at_r.at[1], to_yd)
    at3 = send(attention.at[high], att.at[y, high], at_s.at[3], at_r.at[3], to_yu)
    at5 = send(attention.at[low], att.at[y, low], at_s.at[5], at_r.at[5], to_yd)

    lane = lax.broadcasted_iota(jnp.int32, (PIECE, 128), 1) < 64
    rs, other = [], 1 - xl
    exp_copy.wait()
    for i, zz in enumerate(z_order):
        scale = [scale_of(exp_v[7 * zz + t]) for t in range(7)]
        scale = jnp.concatenate(scale + [jnp.zeros((1, COLS), F32)], axis=0)
        scale = jnp.concatenate([scale, jnp.zeros((8, 64), F32)], axis=1).T[:COLS]

        middles = []
        for h in (2 * i, 2 * i + 1):
            first_col = h % 2 * PIECE
            code_copies[h].wait()

            def tile(t):
                code = codes_v[h % 3, :, 128 * t : 128 * (t + 1)].astype(F32)
                return code * scale[first_col : first_col + PIECE, t : t + 1]

            for t in range(3):
                rows = slice(t * COLS + first_col, t * COLS + first_col + PIECE)
                deltas[2 * zz, rows] = tile(t).astype(BF16)
                deltas[2 * zz + 1, rows] = tile(t + 4).astype(BF16)
            middles.append(tile(3))
            if h + 3 < 8:
                code_copies[h + 3].start()
        top, bottom = middles
        deltas[2 * zz, 3 * COLS :] = jnp.where(lane, top, pltpu.roll(bottom, 64, 1)).astype(BF16)
        deltas[2 * zz + 1, 3 * COLS :] = jnp.where(lane, pltpu.roll(top, 64, 1), bottom).astype(BF16)
        if i == 0:
            pair = send(deltas.at[2 * zz + other], received.at[0], rs_s.at[0], rs_r.at[0], to_xp)
        elif i < 3:
            to = device(x, y, zz, c)
            rs.append(send(deltas.at[2 * zz + other], received.at[i], rs_s.at[i], rs_r.at[i], to))
            k = i + 2
            rs.append(send(deltas.at[2 * zz + xl], received.at[k], rs_s.at[k], rs_r.at[k], to))

    def add(place, slots):
        acc = deltas[place].astype(F32)
        for k in slots:
            acc = acc + received[k].astype(F32)
        deltas[place] = acc.astype(BF16)

    far, near = 2 * z2 + xl, 2 * z + other
    pair.wait_recv()
    add(far, (0,))
    rs.append(send(deltas.at[far], received.at[5], rs_s.at[5], rs_r.at[5], device(x, y, z2, c)))
    rs[0].wait_recv()
    rs[2].wait_recv()
    add(near, (1, 2))
    rs.append(send(deltas.at[near], received.at[6], rs_s.at[6], rs_r.at[6], to_xp))

    for copy in (rs[1], rs[3], rs[4], rs[5]):
        copy.wait_recv()

    def total(rows, size):
        acc = deltas[r, pl.ds(rows, size)].astype(F32)
        for k in range(3, 7):
            acc = acc + received[k, pl.ds(rows, size)].astype(F32)
        return acc

    par_copy.wait()
    mom_copy.wait()

    def outer_step(rows, piece, size):
        outer_grad = piece[:size, :COLS] / 8
        new_momentum = 0.9 * mom_v[rows] + outer_grad
        new_params = par_v[rows] - 0.7 * (outer_grad + 0.9 * new_momentum)
        mom_v[rows] = new_momentum
        par_v[rows] = new_params
        block[rows] = jnp.concatenate(
            [new_params, jnp.zeros((size, 64), F32)], axis=1
        ).astype(BF16)

    fill = jnp.zeros((64, 128), F32)
    for t in range(3):
        piece = jnp.concatenate([total(t * COLS, COLS), fill], axis=0).T
        outer_step(pl.ds(pl.multiple_of(xl * 64 + t * 128, 64), 128), piece, 128)
    packed = total(3 * COLS, PIECE)
    piece = jnp.concatenate([packed, pltpu.roll(packed, 64, 1), fill], axis=0).T
    outer_step(pl.ds(pl.multiple_of((1 - xl) * 384, 64), 64), piece, 64)
    away = pl.ds(pl.multiple_of((1 - c) * PIECE, 16), PIECE)
    swap = send(block.at[away], block_in, sw_s, sw_r, sibling)
    par_save = pltpu.make_async_copy(par_v, params_out, local_sem.at[4])
    mom_save = pltpu.make_async_copy(mom_v, momentum_out, local_sem.at[5])
    par_save.start()
    mom_save.start()
    swap.wait_recv()
    first = c == 0
    seam_lane = lax.broadcasted_iota(jnp.int32, (112, 128), 1) < 64
    lanes = pl.ds(pl.multiple_of(xh * LATE, 128), LATE)
    own_rows = pl.ds(pl.multiple_of(r * COLS + c * PIECE, 16), PIECE)
    for part in range(2):
        ours = block[pl.ds(pl.multiple_of(c * PIECE + part * 112, 16), 112)].astype(F32)
        theirs = block_in[pl.ds(part * 112, 112)].astype(F32)
        left = jnp.where(first, ours, theirs)
        right = pltpu.roll(jnp.where(first, theirs, ours), 64, 1)
        seam = jnp.where(seam_lane, left[:, 384:], right[:, :128])
        rows = pl.ds(pl.multiple_of(r * COLS + c * PIECE + part * 112, 16), 112)
        weight[xh, rows, :384] = left[:, :384].astype(BF16)
        weight[xh, rows, 384:512] = seam.astype(BF16)
        weight[xh, rows, 512:] = right[:, 128 : EARLY - 384].astype(BF16)
        late[y, z, xl, 2 * c + part, :, lanes] = right[:, EARLY - 384 :].astype(BF16)

    def unit(x_, z_, part, lo=0, size=112):
        start = (2 * z_ + lax.rem(x_, 2)) * COLS + c * PIECE + part * 112 + lo
        return weight.at[x_ // 2, pl.ds(pl.multiple_of(start, 16), size)]

    shares = []

    def share(ref):
        k = len(shares)
        shares.append(send(ref, ref, sib_s.at[k], sib_r.at[k], sibling))
        return shares[-1]

    n_x, n_z = [0], [0]

    def along_x(ref, to):
        k = n_x[0]
        n_x[0] += 1
        return send(ref, ref, xs.at[k], xr.at[k], to)

    def along_z(ref, to):
        k = n_z[0]
        n_z[0] += 1
        return send(ref, ref, zs.at[k], zr.at[k], to)

    def late_send(k, ref, to):
        return send(ref, ref, late_s.at[k], late_r.at[k], to)

    to_y2, to_z2, to_x2 = device(x, y2, z, c), device(x, y, z2, c), device(x2, y, z, c)
    mine = pl.ds(pl.multiple_of(2 * c, 2), 2)
    late_y = [
        late_send(k, late.at[y, z, xl, mine, :, lanes], to)
        for k, to in enumerate((to_yu, to_yd, to_y2))
    ]

    XP, XO, ZU, ZD = to_xp, to_xo, to_zu, to_zd
    own_shares, late_shares = [], []
    pz_u = along_z(unit(x, z, 0), ZU)
    pz_d = along_z(unit(x, z, 0), ZD)
    qx_p = along_x(unit(x, z, 1), XP)
    qx_o = along_x(unit(x, z, 1), XO)
    z_units = [z, zd, zu, z2]
    x_units = [x, xp, xo, x2]
    px_p, px_o, qz_u, qz_d = [], [], [], []
    px_p.append(along_x(unit(x, z, 0), XP))
    px_o.append(along_x(unit(x, z, 0), XO))
    qz_u.append(along_z(unit(x, z, 1), ZU))
    qz_d.append(along_z(unit(x, z, 1), ZD))
    own_shares.append(share(weight.at[xh, own_rows]))

    def both(u, d, u_, d_):
        u.append(along_z(u_, ZU))
        d.append(along_z(d_, ZD))

    att_copy.wait()
    at0.wait_recv()
    at2 = send(att.at[yd, low], att.at[yd, low], at_s.at[2], at_r.at[2], to_yu)
    at1.wait_recv()
    at4 = send(att.at[yu, high], att.at[yu, high], at_s.at[4], at_r.at[4], to_yd)

    pz_u.wait_recv()
    pz2_u = along_z(unit(x, zd, 0, 0, 64), ZU)
    px_p.append(along_x(unit(x, zd, 0), XP))
    px_o.append(along_x(unit(x, zd, 0), XO))
    own_shares.append(share(unit(x, zd, 0)))
    pz_d.wait_recv()
    pz2_d = along_z(unit(x, zu, 0, 64, 48), ZD)
    px_p.append(along_x(unit(x, zu, 0), XP))
    px_o.append(along_x(unit(x, zu, 0), XO))
    own_shares.append(share(unit(x, zu, 0)))
    qx_p.wait_recv()
    both(qz_u, qz_d, unit(xp, z, 1), unit(xp, z, 1))
    own_shares.append(share(unit(xp, z, 1)))
    qx_o.wait_recv()
    late_shares.append(share(unit(xo, z, 1)))

    def got_z(j, bucket):
        qz_u[j].wait_recv()
        bucket.append(share(unit(x_units[j], zd, 1)))
        qz_d[j].wait_recv()
        bucket.append(share(unit(x_units[j], zu, 1)))

    def got_x(j):
        px_p[j].wait_recv()
        own_shares.append(share(unit(xp, z_units[j], 0)))
        px_o[j].wait_recv()
        late_shares.append(share(unit(xo, z_units[j], 0)))

    px2, qz2 = [None] * 4, [None] * 4
    got_z(0, own_shares)
    qz2[0] = along_z(unit(x, zd, 1), ZU)
    got_x(0)
    pz2_u.wait_recv()
    pz2_d.wait_recv()
    px_p.append(along_x(unit(x, z2, 0), XP))
    px_o.append(along_x(unit(x, z2, 0), XO))
    own_shares.append(share(unit(x, z2, 0)))
    qx2_o = along_x(unit(xp, z, 1, 0, 64), XO)
    qx2_p = along_x(unit(xo, z, 1, 64, 48), XP)
    got_x(1)
    px2[0] = along_x(unit(xp, z_units[0], 0), XO)
    px2[1] = along_x(unit(xp, z_units[1], 0), XO)
    got_z(1, own_shares)
    qz2[1] = along_z(unit(xp, zu, 1), ZD)
    both(qz_u, qz_d, unit(xo, z, 1), unit(xo, z, 1))
    got_x(2)
    px2[2] = along_x(unit(xo, z_units[2], 0), XP)
    for j in (0, 1):
        qz2[j].wait_recv()
        own_shares.append(share(unit(x_units[j], z2, 1)))
    got_x(3)
    px2[3] = along_x(unit(xo, z_units[3], 0), XP)
    for copy in own_shares:
        copy.wait_recv()

    for copy in (at3, at5):
        copy.wait_recv()

    def place(side, yy):
        columns = xh if side == 0 else 1 - xh
        return pl.ds(pl.multiple_of(yy * 1792 + columns * PAIR, 128), EARLY)

    def finish(side, i, value):
        here = place(side, lax.rem(y + 11 - 2 * i - i // 2, 4))
        for k in range(0, EARLY, 256):
            part = pl.ds(pl.multiple_of(here.start + k, 128), 256)
            total = hid[:, part].astype(F32) + value[:, k : k + 256].astype(F32)
            hid[:, part] = total.astype(BF16)
        pltpu.make_async_copy(
            hid.at[:, here], hidden_out.at[:, here], save_sem.at[side, i]
        ).start()

    def block_copy(side, i, to):
        return pltpu.make_async_remote_copy(
            src_ref=outs.at[side, i],
            dst_ref=got.at[side, i],
            send_sem=os_.at[side, i],
            recv_sem=or_.at[side, i],
            device_id=to,
            device_id_type=MESH,
        )

    def multiply(side, begin, end):
        columns = xh if side == 0 else 1 - xh

        def step(i, carry):
            yy = lax.rem(y + 1 + 2 * i + i // 2, 4)
            result = jnp.dot(att[yy], weight[columns], preferred_element_type=F32).astype(BF16)

            @pl.when(i < 3)
            def _():
                outs[side, i] = result
                block_copy(side, i, device(x, yy, z, c)).start()

            @pl.when(i == 3)
            def _():
                finish(side, i, result)

            return carry

        lax.fori_loop(begin, end, step, 0)

    res_copy.wait()
    for copy in late_y:
        copy.wait_recv()
    late_z = [
        late_send(3 + k, late.at[:, z, xl, 2 * c, :, lanes], to)
        for k, to in enumerate((to_zu, to_zd, to_z2))
    ]
    late_x = [
        late_send(6 + k, late.at[:, z, xl, 2 * c + 1, :, lanes], to)
        for k, to in enumerate((to_xp, to_xo, to_x2))
    ]
    multiply(0, 0, 1)
    qx2_o.wait_recv()
    qx2_p.wait_recv()
    both(qz_u, qz_d, unit(x2, z, 1), unit(x2, z, 1))
    late_shares.append(share(unit(x2, z, 1)))
    got_z(2, late_shares)
    qz2[2] = along_z(unit(xo, zd, 1), ZU)
    multiply(0, 1, 2)
    got_z(3, late_shares)
    qz2[3] = along_z(unit(x2, zu, 1), ZD)
    at2.wait_recv()
    at4.wait_recv()
    multiply(0, 2, 4)
    for copy in late_z:
        copy.wait_recv()
    late_zx = [
        late_send(9 + k, late.at[:, :, xl, 2 * c, :, lanes], to)
        for k, to in enumerate((to_xp, to_xo))
    ]
    late_pairs = [late_send(17, late.at[:, :, xl, 2 * c, :, lanes], sibling)]
    for copy in late_x:
        copy.wait_recv()
    late_xz = [
        late_send(11 + k, late.at[:, z, :, 2 * c + 1], to)
        for k, to in enumerate((to_zu, to_zd))
    ]
    late_pairs.append(late_send(18, late.at[:, z, :, 2 * c + 1], sibling))

    for j in (0, 1, 2, 3):
        px2[j].wait_recv()
        late_shares.append(share(unit(x2, z_units[j], 0)))
    for j in (2, 3):
        qz2[j].wait_recv()
        late_shares.append(share(unit(x_units[j], z2, 1)))
    for copy in late_shares:
        copy.wait_recv()
    multiply(1, 0, 4)

    def late_x_unit(x_, lo, size):
        there = pl.ds(pl.multiple_of(x_ // 2 * LATE, 128), LATE)
        return late.at[:, lo : lo + size, lax.rem(x_, 2), 2 * c, :, there]

    def late_z_unit(z_, lo, size):
        return late.at[lo : lo + size, z_, :, 2 * c + 1]

    late_zx[0].wait_recv()
    fx0 = late_send(13, late_x_unit(xp, 0, 2), to_xo)
    late_pairs.append(late_send(19, late_x_unit(xp, 0, 4), sibling))
    late_zx[1].wait_recv()
    fx1 = late_send(14, late_x_unit(xo, 2, 2), to_xp)
    late_pairs.append(late_send(20, late_x_unit(xo, 0, 4), sibling))
    late_xz[0].wait_recv()
    fz0 = late_send(15, late_z_unit(zd, 0, 2), to_zu)
    late_pairs.append(late_send(21, late_z_unit(zd, 0, 4), sibling))
    late_xz[1].wait_recv()
    fz1 = late_send(16, late_z_unit(zu, 2, 2), to_zd)
    late_pairs.append(late_send(22, late_z_unit(zu, 0, 4), sibling))

    def arrive(side, begin, end):
        def step(i, carry):
            block_copy(side, i, to_yu).wait_recv()
            finish(side, i, got[side, i])
            return carry

        lax.fori_loop(begin, end, step, 0)

    arrive(0, 0, 3)
    for copy in (fx0, fx1):
        copy.wait_recv()
    late_pairs.append(late_send(23, late_x_unit(x2, 0, 4), sibling))
    for copy in (fz0, fz1):
        copy.wait_recv()
    late_pairs.append(late_send(24, late_z_unit(z2, 0, 4), sibling))
    arrive(1, 0, 2)
    for copy in late_pairs:
        copy.wait_recv()

    def late_step(yy, carry):
        result = jnp.zeros((TOK, 2 * LATE), F32)
        for k in range(4):
            result = result + jnp.dot(
                att[y, :, k * PAIR : (k + 1) * PAIR],
                late[yy, k].reshape(PAIR, 2 * LATE),
                preferred_element_type=F32,
            )
        result = result.astype(BF16)
        for k in range(2):
            here = pl.ds(pl.multiple_of(yy * 1792 + k * PAIR + EARLY, 128), LATE)
            value = result[:, k * LATE : (k + 1) * LATE].astype(F32)
            hid[:, here] = (hid[:, here].astype(F32) + value).astype(BF16)
            pltpu.make_async_copy(
                hid.at[:, here], hidden_out.at[:, here], late_save.at[yy, k]
            ).start()
        return carry

    lax.fori_loop(0, 4, late_step, 0)
    arrive(1, 2, 3)

    for copy in pending:
        copy.wait_send()
    par_save.wait()
    mom_save.wait()
    for side in range(2):
        for i in range(4):
            here = place(side, y)
            pltpu.make_async_copy(
                hid.at[:, here], hidden_out.at[:, here], save_sem.at[side, i]
            ).wait()
            if i < 3:
                block_copy(side, i, to_yu).wait_send()
            there = pl.ds(i * 1792 + side * PAIR + EARLY, LATE)
            pltpu.make_async_copy(
                hid.at[:, there], hidden_out.at[:, there], late_save.at[i, side]
            ).wait()


def store(hidden, params, momentum, hidden_out, params_out, momentum_out, sem):
    copies = [
        pltpu.make_async_copy(params, params_out, sem.at[4]),
        pltpu.make_async_copy(momentum, momentum_out, sem.at[5]),
    ]
    for k in range(4):
        rows = pl.ds(k * TOK // 4, TOK // 4)
        copies.append(pltpu.make_async_copy(hidden.at[rows], hidden_out.at[rows], sem.at[k]))
    for copy in copies:
        copy.start()
    for copy in copies:
        copy.wait()


def shards(codes, exponents, params, momentum, attention, residual):
    any_space = pl.BlockSpec(memory_space=pl.ANY)
    dma = pltpu.SemaphoreType.DMA
    outer = jax.ShapeDtypeStruct((COLS, COLS), F32)
    hidden = jax.ShapeDtypeStruct((TOK, 4 * 2 * PAIR), BF16)
    new_params, new_momentum, new_hidden = pl.pallas_call(
        kernel,
        out_shape=(outer, outer, hidden),
        in_specs=[any_space] * 6,
        out_specs=(any_space, any_space, any_space),
        scratch_shapes=[
            pltpu.VMEM((3, PIECE, PAIR), jnp.int32),
            pltpu.VMEM((4 * 7, 1, COLS), jnp.int32),
            pltpu.VMEM((8, SEND, 128), BF16),
            pltpu.VMEM((7, SEND, 128), BF16),
            pltpu.VMEM((COLS, COLS), F32),
            pltpu.VMEM((COLS, COLS), F32),
            pltpu.VMEM((COLS, 512), BF16),
            pltpu.VMEM((PIECE, 512), BF16),
            pltpu.VMEM((2, KDIM, EARLY), BF16),
            pltpu.VMEM((4, 4, 2, 4, 112, 2 * LATE), BF16),
            pltpu.VMEM((4, TOK, KDIM), BF16),
            pltpu.VMEM((2, 3, TOK, EARLY), BF16),
            pltpu.VMEM((2, 3, TOK, EARLY), BF16),
            pltpu.VMEM((TOK, 4 * 2 * PAIR), BF16),
            dma((17,)),
            dma((7,)), dma((7,)),
            dma((6,)), dma((6,)),
            dma, dma,
            dma((31,)), dma((31,)),
            dma((25,)), dma((25,)),
            dma((16,)), dma((16,)),
            dma((16,)), dma((16,)),
            dma((2, 3)), dma((2, 3)),
            dma((2, 4)),
            dma((4, 2)),
        ],
        compiler_params=pltpu.CompilerParams(
            collective_id=0, has_side_effects=True, vmem_limit_bytes=VMEM_LIMIT
        ),
    )(
        jnp.swapaxes(codes[0], 0, 1),
        keep(jnp.swapaxes(exponents, 0, 1)),
        *(keep(a) for a in (params, momentum, attention[0], residual[0])),
    )
    new_hidden, new_params, new_momentum = pl.pallas_call(
        store,
        out_shape=(hidden, outer, outer),
        in_specs=[any_space] * 3,
        out_specs=(any_space, any_space, any_space),
        scratch_shapes=[dma((6,))],
        compiler_params=pltpu.CompilerParams(vmem_limit_bytes=2**20),
    )(new_hidden, new_params, new_momentum)
    return (new_params, new_momentum, new_hidden[None])


def solution(mesh):
    placed = (
        P("replica", None, "fsdp"),
        P("replica", None, "fsdp"),
        P("replica", "fsdp"),
        P("replica", "fsdp"),
        P("replica", "fsdp", None),
        P("replica", "fsdp", None),
    )
    return jax.shard_map(
        shards,
        mesh=mesh,
        in_specs=placed,
        out_specs=(P("replica", "fsdp"), P("replica", "fsdp"), P("replica", "fsdp", None)),
        check_vma=False,
    )
```
